512 devices in a mesh: tm: 256 (over z, y, x), col: 2 (over core).
Axes of the slice: x: 4, y: 8, z: 8, core: 2. Of those that a mesh axis runs over, the one named last changes fastest.
Arguments:
- observations: float32 [1, 256, 256], P(None, 'tm'), may hold values from -6 to 6
- sensor_mask: int32 [1, 256, 256], P(None, 'tm'), may hold values 0 or 1
- filter_gain: float32 [1, 256, 256, 256], P(None, 'tm', 'col'), may hold values from -1 to 1
- smoother_gain: float32 [1, 256, 256, 256], P(None, 'tm', 'col'), may hold values from -1 to 1
- dynamics: float32 [1, 256, 256], replicated, may hold values from -1 to 1
- process_noise: float32 [1, 256, 256], replicated, may hold values from -1 to 1, as said below
- sensor_noise: float32 [1, 256], replicated, may hold values from 0.1 to 4
- initial_mean: float32 [1, 256], replicated, may hold values from -6 to 6
- initial_cov: float32 [1, 256, 256], replicated, may hold values from -2 to 3, as said below
Outputs:
- smoothed_mean: float32 [1, 256, 256], P(None, 'tm', 'col')
- smoothed_cov: float32 [1, 256, 256, 256], P(None, 'tm', 'col')
The draws below stay inside these ranges and needn't reach their ends.
Inputs may be any that keep to these rules, and one draw needn't show every extreme that they name: `process_noise`: symmetric. `initial_cov`: symmetric.
All inputs are finite; a program needn't handle non-finite values. No bound on the sum of `sensor_mask` on one device may be relied on, other than what follows from the above.
Results may differ from the reference program's by a relative error of at most 0.0003.
Values sent between devices are 32-bit elements; how exact they have to be, the bound alone decides.
A program may use at most 64 MiB of HBM per device.

```python
import math
import jax
import jax.numpy as jnp
from jax import lax

STATE = 256
BASINS = 1
STEPS = 256


def log_uniform(key, array_shape, lowest, highest):
    return jnp.exp(jax.random.uniform(key, array_shape, jnp.float32, math.log(lowest), math.log(highest)))


def off_diagonal(key, array_shape):
    order = array_shape[-1]
    values = jax.random.uniform(key, array_shape, jnp.float32, -1.0, 1.0)
    return values * (1.0 - jnp.eye(order, dtype=jnp.float32))


def mixing(key):
    key = jax.random.fold_in(key, 5)
    angle_key, row_key, column_key, sign_key = jax.random.split(key, 4)
    bit_count = STATE.bit_length() - 1
    angles = jax.random.uniform(angle_key, (BASINS, bit_count), jnp.float32, 0.25, 1.3)
    all_cos = jnp.cos(angles)
    all_sin = jnp.sin(angles)
    row_index = jax.vmap(lambda piece_key: jax.random.permutation(piece_key, STATE))(jax.random.split(row_key, BASINS))
    col_index = jax.vmap(lambda piece_key: jax.random.permutation(piece_key, STATE))(jax.random.split(column_key, BASINS))
    row_index = row_index[:, :, None]
    col_index = col_index[:, None, :]
    row_signs = jnp.where(jax.random.bernoulli(sign_key, 0.5, (BASINS, STATE)), 1.0, -1.0).astype(jnp.float32)
    entries = jnp.ones((BASINS, STATE, STATE), jnp.float32)
    for bit_place in range(bit_count):
        row_bit = row_index // 2 ** bit_place % 2
        col_bit = col_index // 2 ** bit_place % 2
        cos_part = all_cos[:, bit_place][:, None, None]
        sin_part = all_sin[:, bit_place][:, None, None]
        factor = jnp.where(row_bit == col_bit, cos_part, jnp.where(row_bit < col_bit, -sin_part, sin_part))
        entries = entries * factor
    return entries * row_signs[:, :, None]


def kernel_cov(key, scales):
    point_key, sign_key = jax.random.split(key)
    points = jax.random.uniform(point_key, (BASINS, STATE, 3), jnp.float32)
    spacing = 0.5 * STATE ** (-1.0 / 3.0)
    squared = jnp.zeros((BASINS, STATE, STATE), jnp.float32)
    for coord in range(3):
        apart = points[:, :, None, coord] - points[:, None, :, coord]
        squared = squared + apart * apart
    distance = jnp.sqrt(squared)
    row_signs = jnp.where(jax.random.bernoulli(sign_key, 0.5, (BASINS, STATE)), 1.0, -1.0).astype(jnp.float32)
    root_scale = jnp.sqrt(scales) * row_signs
    return root_scale[:, :, None] * root_scale[:, None, :] * jnp.exp(-distance / spacing)


def draw_dynamics(key, part):
    mixed = mixing(key)
    key = jax.random.fold_in(key, 11)
    rates = log_uniform(key, (BASINS, STATE), 0.001, 0.05)
    return (1.0 - rates)[:, :, None] * mixed


def draw_filter_gain(key, part):
    key = jax.random.fold_in(key, 23)
    first_key, second_key = jax.random.split(key)
    diagonal = log_uniform(first_key, (BASINS, STEPS, STATE), 0.02, 0.3)
    root_gain = jnp.sqrt(diagonal)
    coupling = off_diagonal(second_key, (BASINS, STEPS, STATE, STATE)) * root_gain[..., :, None] * root_gain[..., None, :] * (0.5 / math.sqrt(STATE))
    return coupling + jnp.eye(STATE, dtype=jnp.float32)[None, None] * diagonal[..., None]


def draw_smoother_gain(key, part):
    mixed = mixing(key)
    key = jax.random.fold_in(key, 37)
    first_key, second_key, third_key, jitter_key, extra_key = jax.random.split(key, 5)
    rates = log_uniform(first_key, (BASINS, 1, STATE), 0.2 / STEPS, min(10.0 / STEPS, 0.45))
    rates = rates * log_uniform(jitter_key, (BASINS, STEPS, STATE), 0.5, 2.0)
    hits = jax.random.uniform(second_key, (BASINS, STEPS, 1), jnp.float32) < 4.0 / STEPS
    factor = jnp.where(hits, jax.random.uniform(third_key, (BASINS, STEPS, 1), jnp.float32, 0.5, 0.8), 1.0)
    diagonal = (1.0 - rates) * factor
    turned = diagonal[..., None] * jnp.swapaxes(mixed, 1, 2)[:, None]
    extra = jax.random.uniform(extra_key, (BASINS, STEPS, STATE, STATE), jnp.float32, -1.0, 1.0) * (0.06 / math.sqrt(STATE))
    return turned + extra


def draw_process_noise(key, part):
    key = jax.random.fold_in(key, 41)
    scale_key, shape_key = jax.random.split(key)
    scales = log_uniform(scale_key, (BASINS, STATE), 0.001, 0.01)
    return kernel_cov(shape_key, scales)


def draw_initial_cov(key, part):
    key = jax.random.fold_in(key, 53)
    scale_key, shape_key = jax.random.split(key)
    scales = log_uniform(scale_key, (BASINS, STATE), 0.2, 2.0)
    return kernel_cov(shape_key, scales)


def with_ends(result, key, low, top_value):
    dims = result.shape
    index_at = [jax.random.randint(jax.random.fold_in(key, axis), (), 0, dims[axis]) for axis in range(len(dims))]
    result = result.at[tuple(index_at)].set(low)
    longest = dims.index(max(dims))
    index_at[longest] = (index_at[longest] + 1) % dims[longest]
    return result.at[tuple(index_at)].set(top_value)


def shard_levels(stream_key, dims, cuts, low, top_value):
    loudness, own = 1.0, jax.random.fold_in(stream_key, 6)
    for axis_at, blocks in cuts:
        heights = jnp.exp(jax.random.uniform(jax.random.fold_in(own, axis_at), (blocks,), jnp.float32, low / len(cuts), top_value / len(cuts)))
        loudness = loudness * jnp.repeat(heights, dims[axis_at] // blocks).reshape([-1 if axis == axis_at else 1 for axis in range(len(dims))])
    return loudness


def bell_draw(key, shape, scale, bound, shards=(), kind=jnp.bfloat16):
    drawn = jax.random.normal(key, shape, jnp.float32) * scale
    if len(shards) > 0:
        drawn = shard_levels(key, shape, shards, -0.22, 0.18) * drawn
    return jnp.clip(drawn, min=-bound, max=bound).astype(kind)


def setup_inputs(seed: int = 0) -> dict:
    streams_of = jax.random.split(jax.random.key(seed), 10)
    observations = bell_draw(streams_of[0], (BASINS, STEPS, STATE), 1.0, 6.0, ((1, 256),), jnp.float32)
    sensor_mask = with_ends((jax.random.randint(streams_of[1], (BASINS, STEPS, STATE), 0, 20) < 1).astype(jnp.int32), jax.random.fold_in(streams_of[1], 1), 0, 1)
    filter_gain = draw_filter_gain(jax.random.fold_in(streams_of[9], 71), 0)
    smoother_gain = draw_smoother_gain(jax.random.fold_in(streams_of[9], 71), 0)
    dynamics = draw_dynamics(jax.random.fold_in(streams_of[9], 71), 0)
    process_noise = draw_process_noise(jax.random.fold_in(streams_of[9], 71), 0)
    sensor_noise = jnp.clip(jnp.exp(jax.random.uniform(streams_of[6], (BASINS, STATE), jnp.float32, math.log(0.1), math.log(4.0))), 0.1, 4.0)
    initial_mean = bell_draw(streams_of[7], (BASINS, STATE), 1.0, 6.0, (), jnp.float32)
    initial_cov = draw_initial_cov(jax.random.fold_in(streams_of[9], 71), 0)
    return {"observations": observations, "sensor_mask": sensor_mask, "filter_gain": filter_gain, "smoother_gain": smoother_gain, "dynamics": dynamics, "process_noise": process_noise, "sensor_noise": sensor_noise, "initial_mean": initial_mean, "initial_cov": initial_cov}


def product(left, right):
    return jnp.matmul(left, right, precision=lax.Precision.HIGHEST)


def one_basin(inputs):
    observed, reported, gains, back_gains, transition, model_noise, obs_noise, mean_zero, cov_zero = inputs
    identity = jnp.eye(STATE, dtype=jnp.float32)

    def forward(carry, items):
        mean, cov = carry
        values, flags, gain = items
        masked = gain * flags.astype(jnp.float32)[None, :]
        keep = identity - masked
        step_map = product(keep, transition)
        mean = product(step_map, mean) + product(masked, values)
        cov = product(product(step_map, cov), step_map.T) + product(product(keep, model_noise), keep.T) + product(masked * obs_noise[None, :], masked.T)
        return (mean, cov), (mean, cov)

    _, (filt_mean, filt_cov) = lax.scan(forward, (mean_zero, cov_zero), (observed, reported, gains))

    def backward(carry, items):
        smooth_mean, smooth_cov = carry
        mean, cov, gain = items
        predicted = product(product(transition, cov), transition.T) + model_noise
        smooth_mean = product(gain, smooth_mean) + mean - product(gain, product(transition, mean))
        smooth_cov = product(product(gain, smooth_cov), gain.T) + cov - product(product(gain, predicted), gain.T)
        return (smooth_mean, smooth_cov), (smooth_mean, smooth_cov)

    _, (back_mean, back_cov) = lax.scan(backward, (filt_mean[-1], filt_cov[-1]), (filt_mean[:-1], filt_cov[:-1], back_gains[:-1]), reverse=True)
    smooth_mean = jnp.concatenate([back_mean, filt_mean[-1:]], axis=0)
    smooth_cov = jnp.concatenate([back_cov, filt_cov[-1:]], axis=0)
    return smooth_mean, smooth_cov


def reference(observations, sensor_mask, filter_gain, smoother_gain, dynamics, process_noise, sensor_noise, initial_mean, initial_cov):
    smoothed_mean, smoothed_cov = lax.map(one_basin, (observations, sensor_mask, filter_gain, smoother_gain, dynamics, process_noise, sensor_noise, initial_mean, initial_cov))
    return smoothed_mean, smoothed_cov
```

```python
import functools

import jax
import jax.numpy as jnp
from jax import lax
from jax.experimental import pallas as pl
from jax.experimental.pallas import tpu as pltpu
from jax.sharding import PartitionSpec as P

MESH = pl.DeviceIdType.MESH
F32 = jnp.float32
N = 256
H = 128


def grid_dims(steps):
    return {256: (4, 8, 8), 8: (2, 2, 2), 4: (2, 2, 1)}[steps]


def parts(a):
    hi = a.astype(jnp.bfloat16)
    lo = (a - hi.astype(F32)).astype(jnp.bfloat16)
    return hi, lo


def mm(a, b, nt=False):
    ah, al = parts(a)
    bh, bl = parts(b)
    dims = (((1,), (1 if nt else 0,)), ((), ()))
    dot = functools.partial(lax.dot_general, dimension_numbers=dims, preferred_element_type=F32)
    return dot(ah, bh) + (dot(ah, bl) + dot(al, bh))


def cong(f, s, c8):
    t = mm(jnp.concatenate([s, c8], 0), f, nt=True)
    return mm(f, t[:N]), t[N:]


def iota(shape, dim):
    return lax.broadcasted_iota(jnp.int32, shape, dim)


def pack(s):
    r, c = iota((H, H), 0), iota((H, H), 1)
    s00, s01, s11 = s[:H, :H], s[:H, H:], s[H:, H:]
    tri = jnp.where(r >= c, s00, s11)
    d11 = jnp.sum(jnp.where(r == c, s11, 0.0), axis=0, keepdims=True)
    fold = lambda m: jnp.concatenate([m[: H // 2], m[H // 2 :]], 1)
    return fold(s01), fold(tri), d11


def unpack(b0, b1, d11):
    r, c = iota((H, H), 0), iota((H, H), 1)
    unfold = lambda m: jnp.concatenate([m[:, :H], m[:, H:]], 0)
    s01, tri = unfold(b0), unfold(b1)
    trit = tri.T
    s00 = jnp.where(r >= c, tri, trit)
    s11 = jnp.where(r == c, d11, jnp.where(r < c, tri, trit))
    top = jnp.concatenate([s00, s01], 1)
    low = jnp.concatenate([s01.T, s11], 1)
    return jnp.concatenate([top, low], 0)


def vec_block(c8, d11):
    d8 = jnp.broadcast_to(jnp.concatenate([jnp.zeros((1, H), F32), d11], 1), (8, N))
    return jnp.where(iota((8, N), 0) == 0, c8, d8)


def rows8(v):
    return jnp.broadcast_to(v, (8, N))


def kernel(dims, obs_ref, mask_ref, fg_ref, sg_ref, a_ref, q_ref, r_ref, m0_ref, p0_ref,
           mean_ref, cov_ref,
           mb, gb, fi, si, ci, yb, yv, zb, zv, ex, by, byv, bz, bzv, gm, lm,
           cf, cs, cc, pf, ps, pc, qf, qs, qc, hx, wy, xa, xc, ca, cv, send_sem, recv_sem):
    nx, ny, nz = dims
    t = lax.axis_index("tm")
    c = lax.axis_index("col")
    o = 1 - c
    x = lax.rem(t, nx)
    y = lax.rem(t // nx, ny)
    z = t // (nx * ny)

    def at_x(d):
        return (t - x + lax.rem(x + d, nx), c)

    def at_y(d):
        return (t - y * nx + lax.rem(y + d, ny) * nx, c)

    def at_z(d):
        return (t - z * (nx * ny) + lax.rem(z + d, nz) * (nx * ny), c)

    sib = (t, o)
    rings = {"x": (at_x, x, nx), "y": (at_y, y, ny), "z": (at_z, z, nz)}

    def order(n):
        out = []
        for d in range(1, n // 2 + 1):
            out.append(d)
            if d != n - d:
                out.append(n - d)
        return out if n > 1 else []

    barrier = pltpu.get_barrier_semaphore()
    peers = [sib]
    for at, _, n in rings.values():
        peers += [at(d) for d in range(1, n)]
    for dev in peers:
        pl.semaphore_signal(barrier, inc=1, device_id=dev, device_id_type=MESH)

    count = [0]
    sent = []

    def slots(k):
        count[0] += k
        return count[0] - k

    def start(ref, sem, dev):
        cp = pltpu.make_async_remote_copy(
            src_ref=ref, dst_ref=ref, send_sem=send_sem.at[sem], recv_sem=recv_sem.at[sem],
            device_id=dev, device_id_type=MESH)
        cp.start()
        sent.append(cp)

    def arrived(ref, sem):
        pltpu.make_async_remote_copy(
            src_ref=ref, dst_ref=ref, send_sem=send_sem.at[sem], recv_sem=recv_sem.at[sem],
            device_id=sib, device_id_type=MESH).wait_recv()

    class Gather:
        def __init__(self, ring, buf):
            self.at, self.me, self.n = rings[ring]
            self.buf = buf
            self.s1, self.s2 = slots(self.n), slots(self.n)

        def source(self, d):
            return lax.rem(self.me + self.n - d, self.n)

        def send(self):
            for d in order(self.n):
                start(self.buf.at[self.me, c], self.s1 + d, self.at(d))

        def swap(self, d):
            if d:
                arrived(self.buf.at[self.source(d), c], self.s1 + d)
            start(self.buf.at[self.source(d), c], self.s2 + d, sib)

        def swapped(self, d):
            arrived(self.buf.at[self.source(d), o], self.s2 + d)

        def finish(self):
            for d in order(self.n):
                self.swap(d)
            for d in order(self.n):
                self.swapped(d)

    class SplitGather:
        def __init__(self, ring, buf, vec):
            self.at, self.me, self.n = rings[ring]
            self.buf, self.vec = buf, vec
            self.s1, self.s2, self.sv = slots(self.n), slots(self.n), slots(self.n)
            self.s3 = slots(self.n * nx)

        def source(self, d):
            return lax.rem(self.me + self.n - d, self.n)

        def send(self):
            for d in order(self.n):
                start(self.buf.at[self.me, c, x], self.s1 + d, self.at(d))
            for d in order(self.n):
                start(self.vec.at[self.me], self.sv + d, self.at(d))

        def forward(self):
            for d in order(self.n):
                k = self.source(d)
                arrived(self.buf.at[k, c, x], self.s1 + d)
                for e in order(nx):
                    start(self.buf.at[k, c, x], self.s3 + d * nx + e, at_x(e))

        def collect(self):
            for d in order(self.n):
                k = self.source(d)
                for e in order(nx):
                    arrived(self.buf.at[k, c, lax.rem(x + nx - e, nx)], self.s3 + d * nx + e)
                start(self.buf.at[k, c], self.s2 + d, sib)
            for d in order(self.n):
                arrived(self.vec.at[self.source(d)], self.sv + d)

        def swapped(self):
            for d in order(self.n):
                arrived(self.buf.at[self.source(d), o], self.s2 + d)

    pr = H // nx
    sr = H // 2 // nx

    def put_item(buf, vec, k, f, s, c8):
        b0, b1, d11 = pack(s)
        for h, blk in ((0, b0), (1, b1)):
            for q in range(nx):
                buf[k, h, q, :pr] = f[h * H + q * pr : h * H + (q + 1) * pr]
                buf[k, h, q, pr:] = blk[q * sr : (q + 1) * sr]
        vec[k] = vec_block(c8, d11)

    def get_item(buf, vec, k):
        f = jnp.concatenate([buf[k, h, q, :pr] for h in range(2) for q in range(nx)], 0)
        b = [jnp.concatenate([buf[k, h, q, pr:] for q in range(nx)], 0) for h in range(2)]
        v = vec[k]
        return f, unpack(b[0], b[1], v[1:2, H:]), rows8(v[0:1])

    def put_sym(buf, vec, k, s, c8):
        b0, b1, d11 = pack(s)
        for h, blk in ((0, b0), (1, b1)):
            for q in range(nx):
                buf[k, h, q] = blk[q * sr : (q + 1) * sr]
        vec[k] = vec_block(c8, d11)

    def get_sym(buf, vec, k):
        b = [jnp.concatenate([buf[k, h, q] for q in range(nx)], 0) for h in range(2)]
        v = vec[k]
        return unpack(b[0], b[1], v[1:2, H:]), rows8(v[0:1])

    def whole(buf, k):
        return jnp.concatenate([buf[k, 0, :H], buf[k, 1, :H]], 0)

    mask = mask_ref[...].astype(F32)
    mb[x, c, :H] = fg_ref[...] * mask
    mb[x, c, H:] = rows8(obs_ref[...])
    gb[x, c] = sg_ref[...]
    pl.semaphore_wait(barrier, len(peers))
    m_ag, g_ag = Gather("x", mb), Gather("x", gb)
    m_ag.swap(0)
    m_ag.send()
    g_ag.swap(0)
    g_ag.send()

    def step_item(d):
        k = m_ag.source(d)
        m = whole(mb, k)
        both = mm(m, jnp.concatenate([a_ref[...], q_ref[...]], 1))
        u = both[:, N:]
        v = u + m * r_ref[...] - q_ref[...]
        w = mm(jnp.concatenate([v, mb[k, c, H:]], 0), m, nt=True)
        fi[k] = a_ref[...] - both[:, :N]
        si[k] = q_ref[...] - u + w[:N]
        ci[k] = w[N:]

    m_ag.swapped(0)
    step_item(0)
    for d in order(nx):
        m_ag.swap(d)
        m_ag.swapped(d)
        step_item(d)

    eye = jnp.where(iota((N, N), 0) == iota((N, N), 1), 1.0, 0.0).astype(F32)
    zero8 = jnp.zeros((8, N), F32)
    pf[...] = eye
    ps[...] = jnp.zeros((N, N), F32)
    pc[...] = zero8
    cf[...] = fi[0]
    cs[...] = si[0]
    cc[...] = ci[0]

    def chain(steps, me, item, f_ref, s_ref, c_ref):
        def body(k, carry):
            @pl.when(me == k)
            def _():
                f_ref[...] = cf[...]
                s_ref[...] = cs[...]
                c_ref[...] = cc[...]

            f, s, c8 = item(k)
            ns, nc = cong(f, cs[...], cc[...])
            cf[...] = mm(f, cf[...])
            cs[...] = ns + s
            cc[...] = nc + c8
            return carry

        lax.fori_loop(1, steps, body, 0)

    chain(nx, x, lambda k: (fi[k], si[k], ci[k]), pf, ps, pc)

    y_ag = SplitGather("y", yb, yv)
    put_item(yb, yv, y, cf[...], cs[...], cc[...])
    y_ag.send()

    g_ag.swapped(0)
    g_ag.finish()
    hx[...] = whole(gb, nx - 1)
    cf[...] = whole(gb, nx - 1)

    def back_x(i, carry):
        k = nx - 2 - i
        cf[...] = mm(whole(gb, k), cf[...])

        @pl.when(x == k)
        def _():
            hx[...] = cf[...]

        return carry

    lax.fori_loop(0, nx - 1, back_x, 0)
    gm[y, 0] = cf[:H]
    gm[y, 1] = cf[H:]

    y_ag.forward()
    y_ag.collect()
    y_ag.swapped()
    qf[...] = eye
    qs[...] = jnp.zeros((N, N), F32)
    qc[...] = zero8
    f0, s0, c0 = get_item(yb, yv, 0)
    cf[...] = f0
    cs[...] = s0
    cc[...] = c0
    chain(ny, y, lambda k: get_item(yb, yv, k), qf, qs, qc)

    z_ag = SplitGather("z", zb, zv)
    put_item(zb, zv, z, cf[...], cs[...], cc[...])
    z_ag.send()
    gm_ag = Gather("y", gm)
    gm_ag.send()
    ns, nc = cong(pf[...], qs[...], qc[...])
    qf[...] = mm(pf[...], qf[...])
    qs[...] = ns + ps[...]
    qc[...] = nc + pc[...]
    z_ag.forward()
    z_ag.collect()
    z_ag.swapped()
    cs[...] = p0_ref[...]
    cc[...] = rows8(m0_ref[...])

    def carry_in(k, carry):
        f, s, c8 = get_item(zb, zv, k)
        ns, nc = cong(f, cs[...], cc[...])
        cs[...] = ns + s
        cc[...] = nc + c8
        return carry

    lax.fori_loop(0, z, carry_in, 0)
    p_prev, m_prev = cong(qf[...], cs[...], cc[...])
    p_prev = p_prev + qs[...]
    m_prev = m_prev + qc[...]

    pred, am = cong(a_ref[...], p_prev, m_prev)
    pred = pred + q_ref[...]
    m = whole(mb, x)
    w = mm(m, pred)
    v = w + m * r_ref[...] - pred
    ee = mm(jnp.concatenate([v, rows8(obs_ref[...]) - am], 0), m, nt=True)
    e_cov = ee[:N] - w
    e_vec = ee[N:]
    b0, b1, d11 = pack(e_cov)
    vb = vec_block(e_vec, d11)
    for h, blk in ((0, b0), (1, b1)):
        ex[x, h, : H // 2] = blk
        ex[x, h, H // 2 :] = vb
    ps[...] = pred
    pc[...] = am

    e_ag = Gather("x", ex)
    e_ag.send()
    gm_ag.finish()
    wy[...] = eye
    cf[...] = whole(gm, ny - 1)

    def back_y_map(i, carry):
        k = ny - 2 - i

        @pl.when(y == k)
        def _():
            wy[...] = cf[...]

        cf[...] = mm(whole(gm, k), cf[...])
        return carry

    lax.fori_loop(0, ny - 1, back_y_map, 0)
    lm[z, 0] = cf[:H]
    lm[z, 1] = cf[H:]
    lm_ag = Gather("z", lm)
    lm_ag.send()
    e_ag.finish()

    def get_e(k):
        vb = ex[k, c, H // 2 :]
        return unpack(ex[k, 0, : H // 2], ex[k, 1, : H // 2], vb[1:2, H:]), rows8(vb[0:1])

    s, c8 = get_e(nx - 1)
    xa[...] = s
    xc[...] = c8
    cs[...] = s
    cc[...] = c8

    def back_x_cov(i, carry):
        k = nx - 2 - i
        s, c8 = get_e(k)
        ns, nc = cong(whole(gb, k), cs[...], cc[...])
        cs[...] = ns + s
        cc[...] = nc + c8

        @pl.when(x == k)
        def _():
            xa[...] = cs[...]
            xc[...] = cc[...]

        return carry

    lax.fori_loop(0, nx - 1, back_x_cov, 0)

    by_ag = SplitGather("y", by, byv)
    put_sym(by, byv, y, cs[...], cc[...])
    by_ag.send()
    by_ag.forward()
    by_ag.collect()
    by_ag.swapped()
    s, c8 = get_sym(by, byv, ny - 1)
    cs[...] = s
    cc[...] = c8
    ca[...] = jnp.zeros((N, N), F32)
    cv[...] = zero8

    def back_y_cov(i, carry):
        k = ny - 2 - i

        @pl.when(y == k)
        def _():
            ca[...] = cs[...]
            cv[...] = cc[...]

        s, c8 = get_sym(by, byv, k)
        ns, nc = cong(whole(gm, k), cs[...], cc[...])
        cs[...] = ns + s
        cc[...] = nc + c8
        return carry

    lax.fori_loop(0, ny - 1, back_y_cov, 0)

    bz_ag = SplitGather("z", bz, bzv)
    put_sym(bz, bzv, z, cs[...], cc[...])
    bz_ag.send()
    lm_ag.finish()
    ns, nc = cong(hx[...], ca[...], cv[...])
    xa[...] = xa[...] + ns
    xc[...] = xc[...] + nc
    hx[...] = mm(hx[...], wy[...])
    bz_ag.forward()
    bz_ag.collect()
    bz_ag.swapped()
    cs[...] = jnp.zeros((N, N), F32)
    cc[...] = zero8

    def back_z_cov(i, carry):
        k = nz - 1 - i
        s, c8 = get_sym(bz, bzv, k)
        ns, nc = cong(whole(lm, k), cs[...], cc[...])
        cs[...] = ns + s
        cc[...] = nc + c8
        return carry

    lax.fori_loop(0, nz - 1 - z, back_z_cov, 0)
    ns, nc = cong(hx[...], cs[...], cc[...])
    xa[...] = xa[...] + ns + ps[...]
    xc[...] = xc[...] + nc + pc[...]

    cov_ref[...] = xa[pl.ds(pl.multiple_of(c * H, H), H)]
    mean_ref[...] = jnp.where(c == 0, xc[0:1, :H], xc[0:1, H:])
    for cp in sent:
        cp.wait_send()


def shards(steps, observations, sensor_mask, filter_gain, smoother_gain, dynamics, process_noise,
           sensor_noise, initial_mean, initial_cov):
    dims = grid_dims(steps)
    nx, ny, nz = dims
    mat = pltpu.VMEM((N, N), F32)
    vec = pltpu.VMEM((8, N), F32)
    buf = lambda *s: pltpu.VMEM(s + (N,), F32)
    n_sem = 3 * nx * 2 + (ny + nz) * 2 + 2 * (ny + nz) * (3 + nx)
    vmem = pl.BlockSpec(memory_space=pltpu.VMEM)
    mean, cov = pl.pallas_call(
        functools.partial(kernel, dims),
        out_shape=(jax.ShapeDtypeStruct((1, H), F32), jax.ShapeDtypeStruct((H, N), F32)),
        in_specs=[vmem] * 9,
        out_specs=(vmem, vmem),
        scratch_shapes=[
            buf(nx, 2, H + 8), buf(nx, 2, H),
            buf(nx, N), buf(nx, N), buf(nx, 8),
            buf(ny, 2, nx, (H + H // 2) // nx), buf(ny, 8),
            buf(nz, 2, nx, (H + H // 2) // nx), buf(nz, 8),
            buf(nx, 2, H // 2 + 8),
            buf(ny, 2, nx, H // 2 // nx), buf(ny, 8),
            buf(nz, 2, nx, H // 2 // nx), buf(nz, 8),
            buf(ny, 2, H), buf(nz, 2, H),
            mat, mat, vec, mat, mat, vec, mat, mat, vec, mat, mat, mat, vec, mat, vec,
            pltpu.SemaphoreType.DMA((n_sem,)), pltpu.SemaphoreType.DMA((n_sem,)),
        ],
        compiler_params=pltpu.CompilerParams(
            collective_id=0, has_side_effects=True, vmem_limit_bytes=48 << 20),
    )(observations[0], sensor_mask[0], filter_gain[0, 0], smoother_gain[0, 0], dynamics[0],
      process_noise[0], sensor_noise, initial_mean, initial_cov[0])
    return mean[None], cov[None, None]


def solution(mesh):
    return jax.shard_map(
        functools.partial(shards, mesh.shape["tm"]),
        mesh=mesh,
        in_specs=(
            P(None, "tm", None),
            P(None, "tm", None),
            P(None, "tm", "col", None),
            P(None, "tm", "col", None),
            P(),
            P(),
            P(),
            P(),
            P(),
        ),
        out_specs=(P(None, "tm", "col"), P(None, "tm", "col", None)),
        check_vma=False,
    )
```

```python
import functools

import jax
import jax.numpy as jnp
from jax import lax
from jax.experimental import pallas as pl
from jax.experimental.pallas import tpu as pltpu
from jax.sharding import PartitionSpec as P

MESH = pl.DeviceIdType.MESH
F32 = jnp.float32
N = 256
H = 128


def grid_dims(steps):
    return {256: (4, 8, 8), 8: (2, 2, 2), 4: (2, 2, 1)}[steps]


def parts(a):
    hi = a.astype(jnp.bfloat16)
    lo = (a - hi.astype(F32)).astype(jnp.bfloat16)
    return hi, lo


def mm(a, b, nt=False):
    ah, al = parts(a)
    bh, bl = parts(b)
    dims = (((1,), (1 if nt else 0,)), ((), ()))
    dot = functools.partial(lax.dot_general, dimension_numbers=dims, preferred_element_type=F32)
    return dot(ah, bh) + (dot(ah, bl) + dot(al, bh))


def cong(f, s, c8):
    t = mm(jnp.concatenate([s, c8], 0), f, nt=True)
    return mm(f, t[:N]), t[N:]


def iota(shape, dim):
    return lax.broadcasted_iota(jnp.int32, shape, dim)


def pack(s):
    r, c = iota((H, H), 0), iota((H, H), 1)
    s00, s01, s11 = s[:H, :H], s[:H, H:], s[H:, H:]
    tri = jnp.where(r >= c, s00, s11)
    d11 = jnp.sum(jnp.where(r == c, s11, 0.0), axis=0, keepdims=True)
    fold = lambda m: jnp.concatenate([m[: H // 2], m[H // 2 :]], 1)
    return fold(s01), fold(tri), d11


def unpack(b0, b1, d11):
    r, c = iota((H, H), 0), iota((H, H), 1)
    unfold = lambda m: jnp.concatenate([m[:, :H], m[:, H:]], 0)
    s01, tri = unfold(b0), unfold(b1)
    trit = tri.T
    s00 = jnp.where(r >= c, tri, trit)
    s11 = jnp.where(r == c, d11, jnp.where(r < c, tri, trit))
    top = jnp.concatenate([s00, s01], 1)
    low = jnp.concatenate([s01.T, s11], 1)
    return jnp.concatenate([top, low], 0)


def vec_block(c8, d11):
    d8 = jnp.broadcast_to(jnp.concatenate([jnp.zeros((1, H), F32), d11], 1), (8, N))
    return jnp.where(iota((8, N), 0) == 0, c8, d8)


def rows8(v):
    return jnp.broadcast_to(v, (8, N))


def kernel(dims, obs_ref, mask_ref, r_ref, m0_ref, fg_hbm, sg_hbm, a_hbm, q_hbm, p0_hbm,
           mean_ref, cov_ref,
           a_ref, q_ref, p0_ref, mb, gb, fi, si, ci, yb, yv, zb, zv, ex, by, byv, bz, bzv, sb, tb, jb, gm, lm,
           cf, cs, cc, pf, ps, pc, qf, qs, qc, hx, wy, ly, xa, xc, ca, cv, uf, rf, uc,
           send_sem, recv_sem, load_sem):
    nx, ny, nz = dims
    t = lax.axis_index("tm")
    c = lax.axis_index("col")
    o = 1 - c
    x = lax.rem(t, nx)
    y = lax.rem(t // nx, ny)
    z = t // (nx * ny)

    def at_x(d):
        return (t - x + lax.rem(x + d, nx), c)

    def at_y(d):
        return (t - y * nx + lax.rem(y + d, ny) * nx, c)

    def at_z(d):
        return (t - z * (nx * ny) + lax.rem(z + d, nz) * (nx * ny), c)

    sib = (t, o)
    rings = {"x": (at_x, x, nx), "y": (at_y, y, ny), "z": (at_z, z, nz)}

    def order(n):
        out = []
        for d in range(1, n // 2 + 1):
            out.append(d)
            if d != n - d:
                out.append(n - d)
        return out if n > 1 else []

    def load(i, src, dst):
        cp = pltpu.make_async_copy(src, dst, load_sem.at[i])
        cp.start()
        return cp

    barrier = pltpu.get_barrier_semaphore()
    peers = [sib]
    for at, _, n in rings.values():
        peers += [at(d) for d in range(1, n)]
    for dev in peers:
        pl.semaphore_signal(barrier, inc=1, device_id=dev, device_id_type=MESH)

    fg_load = load(0, fg_hbm, mb.at[x, c, pl.ds(0, H)])
    sg_load = load(1, sg_hbm, gb.at[x, c])
    other_loads = [load(2, a_hbm, a_ref), load(3, q_hbm, q_ref), load(4, p0_hbm, p0_ref)]

    count = [0]
    sent = []

    def slots(k):
        count[0] += k
        return count[0] - k

    def start(ref, sem, dev):
        cp = pltpu.make_async_remote_copy(
            src_ref=ref, dst_ref=ref, send_sem=send_sem.at[sem], recv_sem=recv_sem.at[sem],
            device_id=dev, device_id_type=MESH)
        cp.start()
        sent.append(cp)

    def arrived(ref, sem):
        pltpu.make_async_remote_copy(
            src_ref=ref, dst_ref=ref, send_sem=send_sem.at[sem], recv_sem=recv_sem.at[sem],
            device_id=sib, device_id_type=MESH).wait_recv()

    class Gather:
        def __init__(self, ring, buf):
            self.at, self.me, self.n = rings[ring]
            self.buf = buf
            self.s1, self.s2 = slots(self.n), slots(self.n)

        def source(self, d):
            return lax.rem(self.me + self.n - d, self.n)

        def send(self):
            for d in order(self.n):
                start(self.buf.at[self.me, c], self.s1 + d, self.at(d))

        def swap(self, d):
            if d:
                arrived(self.buf.at[self.source(d), c], self.s1 + d)
            start(self.buf.at[self.source(d), c], self.s2 + d, sib)

        def swapped(self, d):
            arrived(self.buf.at[self.source(d), o], self.s2 + d)

        def finish(self):
            for d in order(self.n):
                self.swap(d)
            for d in order(self.n):
                self.swapped(d)

    class SplitGather:
        def __init__(self, ring, buf, vec):
            self.at, self.me, self.n = rings[ring]
            self.buf, self.vec = buf, vec
            self.s1, self.s2, self.sv = slots(self.n), slots(self.n), slots(self.n)
            self.s3 = slots(self.n * nx)

        def source(self, d):
            return lax.rem(self.me + self.n - d, self.n)

        def send(self):
            for d in order(self.n):
                start(self.buf.at[self.me, c, x], self.s1 + d, self.at(d))
            for d in order(self.n):
                start(self.vec.at[self.me], self.sv + d, self.at(d))

        def forward(self):
            for d in order(self.n):
                k = self.source(d)
                arrived(self.buf.at[k, c, x], self.s1 + d)
                for e in order(nx):
                    start(self.buf.at[k, c, x], self.s3 + d * nx + e, at_x(e))

        def collect(self):
            for d in order(self.n):
                k = self.source(d)
                for e in order(nx):
                    arrived(self.buf.at[k, c, lax.rem(x + nx - e, nx)], self.s3 + d * nx + e)
                start(self.buf.at[k, c], self.s2 + d, sib)
            for d in order(self.n):
                arrived(self.vec.at[self.source(d)], self.sv + d)

        def swapped_one(self, d):
            arrived(self.buf.at[self.source(d), o], self.s2 + d)

        def swapped(self):
            for d in order(self.n):
                self.swapped_one(d)

    pr = H // nx
    sr = H // 2 // nx

    def put_item(buf, vec, k, f, s, c8):
        b0, b1, d11 = pack(s)
        for h, blk in ((0, b0), (1, b1)):
            for q in range(nx):
                buf[k, h, q, :pr] = f[h * H + q * pr : h * H + (q + 1) * pr]
                buf[k, h, q, pr:] = blk[q * sr : (q + 1) * sr]
        vec[k] = vec_block(c8, d11)

    def get_item(buf, vec, k):
        f = jnp.concatenate([buf[k, h, q, :pr] for h in range(2) for q in range(nx)], 0)
        b = [jnp.concatenate([buf[k, h, q, pr:] for q in range(nx)], 0) for h in range(2)]
        v = vec[k]
        return f, unpack(b[0], b[1], v[1:2, H:]), rows8(v[0:1])

    def put_sym(buf, vec, k, s, c8):
        b0, b1, d11 = pack(s)
        for h, blk in ((0, b0), (1, b1)):
            for q in range(nx):
                buf[k, h, q] = blk[q * sr : (q + 1) * sr]
        vec[k] = vec_block(c8, d11)

    def get_sym(buf, vec, k):
        b = [jnp.concatenate([buf[k, h, q] for q in range(nx)], 0) for h in range(2)]
        v = vec[k]
        return unpack(b[0], b[1], v[1:2, H:]), rows8(v[0:1])

    def whole(buf, k):
        return jnp.concatenate([buf[k, 0, :H], buf[k, 1, :H]], 0)

    mask = mask_ref[...].astype(F32)
    mb[x, c, H:] = rows8(obs_ref[...])
    fg_load.wait()
    mb[x, c, :H] = mb[x, c, :H] * mask
    pl.semaphore_wait(barrier, len(peers))
    m_ag, g_ag = Gather("x", mb), Gather("x", gb)
    m_ag.send()
    m_ag.swap(0)

    def step_item(d):
        k = m_ag.source(d)
        m = whole(mb, k)
        both = mm(m, jnp.concatenate([a_ref[...], q_ref[...]], 1))
        u = both[:, N:]
        v = u + m * r_ref[...] - q_ref[...]
        w = mm(jnp.concatenate([v, mb[k, c, H:]], 0), m, nt=True)
        fi[k] = a_ref[...] - both[:, :N]
        si[k] = q_ref[...] - u + w[:N]
        ci[k] = w[N:]

    for cp in other_loads:
        cp.wait()
    m_ag.swapped(0)
    step_item(0)
    for d in order(nx):
        m_ag.swap(d)
        if d == order(nx)[-1]:
            sg_load.wait()
            g_ag.swap(0)
            g_ag.send()
        m_ag.swapped(d)
        step_item(d)

    eye = jnp.where(iota((N, N), 0) == iota((N, N), 1), 1.0, 0.0).astype(F32)
    zero8 = jnp.zeros((8, N), F32)
    pf[...] = eye
    ps[...] = jnp.zeros((N, N), F32)
    pc[...] = zero8
    cf[...] = fi[0]
    cs[...] = si[0]
    cc[...] = ci[0]

    def chain(steps, me, item, f_ref, s_ref, c_ref):
        def body(k, carry):
            @pl.when(me == k)
            def _():
                f_ref[...] = cf[...]
                s_ref[...] = cs[...]
                c_ref[...] = cc[...]

            f, s, c8 = item(k)
            ns, nc = cong(f, cs[...], cc[...])
            cf[...] = mm(f, cf[...])
            cs[...] = ns + s
            cc[...] = nc + c8
            return carry

        lax.fori_loop(1, steps, body, 0)

    chain(nx, x, lambda k: (fi[k], si[k], ci[k]), pf, ps, pc)

    y_ag = SplitGather("y", yb, yv)
    put_item(yb, yv, y, cf[...], cs[...], cc[...])
    y_ag.send()

    g_ag.swapped(0)
    g_ag.finish()
    hx[...] = whole(gb, nx - 1)
    cf[...] = whole(gb, nx - 1)

    def back_x(i, carry):
        k = nx - 2 - i
        cf[...] = mm(whole(gb, k), cf[...])

        @pl.when(x == k)
        def _():
            hx[...] = cf[...]

        return carry

    lax.fori_loop(0, nx - 1, back_x, 0)
    gm[y, 0] = cf[:H]
    gm[y, 1] = cf[H:]

    y_ag.forward()
    gm_ag = Gather("y", gm)
    gm_ag.send()
    y_ag.collect()
    y_ag.swapped()

    cf[...] = eye
    cs[...] = jnp.zeros((N, N), F32)
    cc[...] = zero8
    rf[...] = eye
    uf[...] = jnp.zeros((N, N), F32)
    uc[...] = zero8

    def add_term():
        term = mm(jnp.concatenate([uf[...], uc[...]], 0), rf[...], nt=True)
        cs[...] += term[:N]
        cc[...] += term[N:]

    def total_y(i, carry):
        f, s, c8 = get_item(yb, yv, ny - 1 - i)
        r = cf[...]
        both = mm(r, jnp.concatenate([f, s], 1))
        add_term()
        rf[...] = r
        uf[...] = both[:, N:]
        uc[...] = c8
        cf[...] = both[:, :N]
        return carry

    lax.fori_loop(0, ny, total_y, 0)
    add_term()

    z_ag = SplitGather("z", zb, zv)
    put_item(zb, zv, z, cf[...], cs[...], cc[...])
    z_ag.send()

    qf[...] = eye
    qs[...] = jnp.zeros((N, N), F32)
    qc[...] = zero8

    def before(f, s, c8):
        ns, nc = cong(f, qs[...], qc[...])
        qf[...] = mm(f, qf[...])
        qs[...] = ns + s
        qc[...] = nc + c8

    def before_y(k, carry):
        before(*get_item(yb, yv, k))
        return carry

    lax.fori_loop(0, y, before_y, 0)
    before(pf[...], ps[...], pc[...])
    z_ag.forward()

    gm_ag.finish()
    cf[...] = eye

    def map_y(k, carry):
        @pl.when(y == k)
        def _():
            ly[...] = cf[...]

        cf[...] = mm(cf[...], whole(gm, k))
        return carry

    lax.fori_loop(0, ny, map_y, 0)
    lm[z, 0] = cf[:H]
    lm[z, 1] = cf[H:]
    lm_ag = Gather("z", lm)
    lm_ag.send()

    z_ag.collect()
    z_ag.swapped()
    cs[...] = p0_ref[...]
    cc[...] = rows8(m0_ref[...])

    def carry_in(k, carry):
        f, s, c8 = get_item(zb, zv, k)
        ns, nc = cong(f, cs[...], cc[...])
        cs[...] = ns + s
        cc[...] = nc + c8
        return carry

    lax.fori_loop(0, z, carry_in, 0)
    p_prev, m_prev = cong(qf[...], cs[...], cc[...])
    p_prev = p_prev + qs[...]
    m_prev = m_prev + qc[...]

    pred, am = cong(a_ref[...], p_prev, m_prev)
    pred = pred + q_ref[...]
    m = whole(mb, x)
    w = mm(m, pred)
    v = w + m * r_ref[...] - pred
    ee = mm(jnp.concatenate([v, rows8(obs_ref[...]) - am], 0), m, nt=True)
    e_cov = ee[:N] - w
    e_vec = ee[N:]
    b0, b1, d11 = pack(e_cov)
    vb = vec_block(e_vec, d11)
    for h, blk in ((0, b0), (1, b1)):
        ex[x, h, : H // 2] = blk
        ex[x, h, H // 2 :] = vb
    ps[...] = pred
    pc[...] = am

    e_ag = Gather("x", ex)
    e_ag.send()
    cf[...] = eye

    def back_y_map(i, carry):
        k = ny - 1 - i

        @pl.when(y == k)
        def _():
            wy[...] = cf[...]

        cf[...] = mm(whole(gm, k), cf[...])
        return carry

    lax.fori_loop(0, ny - 1, back_y_map, 0)

    @pl.when(y == 0)
    def _():
        wy[...] = cf[...]

    rf[...] = mm(hx[...], wy[...])
    e_ag.finish()

    def get_e(k):
        vb = ex[k, c, H // 2 :]
        return unpack(ex[k, 0, : H // 2], ex[k, 1, : H // 2], vb[1:2, H:]), rows8(vb[0:1])

    s, c8 = get_e(nx - 1)
    xa[...] = s
    xc[...] = c8
    cs[...] = s
    cc[...] = c8

    def back_x_cov(i, carry):
        k = nx - 2 - i
        s, c8 = get_e(k)
        ns, nc = cong(whole(gb, k), cs[...], cc[...])
        cs[...] = ns + s
        cc[...] = nc + c8

        @pl.when(x == k)
        def _():
            xa[...] = cs[...]
            xc[...] = cc[...]

        return carry

    lax.fori_loop(0, nx - 1, back_x_cov, 0)

    ns, nc = cong(ly[...], cs[...], cc[...])
    b0, b1, d11 = pack(ns)
    for h, blk in ((0, b0), (1, b1)):
        for q in range(nx):
            tb[h, q] = blk[q * sr : (q + 1) * sr]
    sb[y, :sr] = tb[c, x]
    sb[y, sr:] = vec_block(nc, d11)
    s_slots = slots(ny)
    for d in order(ny):
        start(sb.at[y], s_slots + d, at_y(d))
    by_ag = SplitGather("y", by, byv)
    put_sym(by, byv, y, cs[...], cc[...])
    by_ag.send()

    lm_ag.finish()
    cf[...] = rf[...]

    def map_z(k, carry):
        jb[k] = cf[...]
        cf[...] = mm(cf[...], whole(lm, k))
        return carry

    lax.fori_loop(z + 1, nz, map_z, 0)

    for d in order(ny):
        arrived(sb.at[by_ag.source(d)], s_slots + d)
    total = sb[0]
    for k in range(1, ny):
        total = total + sb[k]
    bz_ag = SplitGather("z", bz, bzv)
    bz[z, c, x] = total[:sr]
    bzv[z] = total[sr:]
    bz_ag.send()

    by_ag.forward()
    by_ag.collect()
    bz_ag.forward()
    by_ag.swapped()
    ca[...] = jnp.zeros((N, N), F32)
    cv[...] = zero8

    def back_y_cov(i, carry):
        k = ny - 1 - i
        s, c8 = get_sym(by, byv, k)
        ns, nc = cong(whole(gm, k), ca[...], cv[...])
        ca[...] = ns + s
        cv[...] = nc + c8
        return carry

    lax.fori_loop(0, ny - 1 - y, back_y_cov, 0)
    ns, nc = cong(hx[...], ca[...], cv[...])
    xa[...] = xa[...] + ns + ps[...]
    xc[...] = xc[...] + nc + pc[...]

    bz_ag.collect()
    for d in order(nz):
        k = bz_ag.source(d)
        bz_ag.swapped_one(d)

        @pl.when(k > z)
        def _():
            s, c8 = get_sym(bz, bzv, k)
            ns, nc = cong(jb[k], s, c8)
            xa[...] += ns
            xc[...] += nc

    cov_ref[...] = xa[pl.ds(pl.multiple_of(c * H, H), H)]
    mean_ref[...] = jnp.where(c == 0, xc[0:1, :H], xc[0:1, H:])
    for cp in sent:
        cp.wait_send()


def shards(steps, observations, sensor_mask, filter_gain, smoother_gain, dynamics, process_noise,
           sensor_noise, initial_mean, initial_cov):
    dims = grid_dims(steps)
    nx, ny, nz = dims
    mat = pltpu.VMEM((N, N), F32)
    vec = pltpu.VMEM((8, N), F32)
    buf = lambda *s: pltpu.VMEM(s + (N,), F32)
    n_sem = 3 * nx * 2 + (ny + nz) * 2 + 2 * (ny + nz) * (3 + nx) + ny
    vmem = pl.BlockSpec(memory_space=pltpu.VMEM)
    hbm = pl.BlockSpec(memory_space=pltpu.HBM)
    sr = H // 2 // nx
    mean, cov = pl.pallas_call(
        functools.partial(kernel, dims),
        out_shape=(jax.ShapeDtypeStruct((1, H), F32), jax.ShapeDtypeStruct((H, N), F32)),
        in_specs=[vmem] * 4 + [hbm] * 5,
        out_specs=(vmem, vmem),
        scratch_shapes=[
            mat, mat, mat,
            buf(nx, 2, H + 8), buf(nx, 2, H),
            buf(nx, N), buf(nx, N), buf(nx, 8),
            buf(ny, 2, nx, (H + H // 2) // nx), buf(ny, 8),
            buf(nz, 2, nx, (H + H // 2) // nx), buf(nz, 8),
            buf(nx, 2, H // 2 + 8),
            buf(ny, 2, nx, H // 2 // nx), buf(ny, 8),
            buf(nz, 2, nx, H // 2 // nx), buf(nz, 8),
            buf(ny, sr + 8), buf(2, nx, sr), buf(nz, N), buf(ny, 2, H), buf(nz, 2, H),
            mat, mat, vec, mat, mat, vec, mat, mat, vec, mat, mat, mat, mat, vec, mat, vec,
            mat, mat, vec,
            pltpu.SemaphoreType.DMA((n_sem,)), pltpu.SemaphoreType.DMA((n_sem,)),
            pltpu.SemaphoreType.DMA((5,)),
        ],
        compiler_params=pltpu.CompilerParams(
            collective_id=0, has_side_effects=True, vmem_limit_bytes=60 << 20),
    )(observations[0], sensor_mask[0], sensor_noise, initial_mean, filter_gain[0, 0],
      smoother_gain[0, 0], dynamics[0], process_noise[0], initial_cov[0])
    return mean[None], cov[None, None]


def solution(mesh):
    return jax.shard_map(
        functools.partial(shards, mesh.shape["tm"]),
        mesh=mesh,
        in_specs=(
            P(None, "tm", None),
            P(None, "tm", None),
            P(None, "tm", "col", None),
            P(None, "tm", "col", None),
            P(),
            P(),
            P(),
            P(),
            P(),
        ),
        out_specs=(P(None, "tm", "col"), P(None, "tm", "col", None)),
        check_vma=False,
    )
```

```python
import functools

import jax
import jax.numpy as jnp
from jax import lax
from jax.experimental import pallas as pl
from jax.experimental.pallas import tpu as pltpu
from jax.sharding import PartitionSpec as P

MESH = pl.DeviceIdType.MESH
F32 = jnp.float32
N = 256
H = 128


def grid_dims(steps):
    return {256: (4, 8, 8), 8: (2, 2, 2), 4: (2, 2, 1)}[steps]


def parts(a):
    hi = a.astype(jnp.bfloat16)
    lo = (a - hi.astype(F32)).astype(jnp.bfloat16)
    return hi, lo


def mm(a, b, nt=False):
    ah, al = parts(a)
    bh, bl = parts(b)
    dims = (((1,), (1 if nt else 0,)), ((), ()))
    dot = functools.partial(lax.dot_general, dimension_numbers=dims, preferred_element_type=F32)
    return dot(ah, bh) + (dot(ah, bl) + dot(al, bh))


def cong(f, s, c8):
    t = mm(jnp.concatenate([s, c8], 0), f, nt=True)
    return mm(f, t[:N]), t[N:]


def iota(shape, dim):
    return lax.broadcasted_iota(jnp.int32, shape, dim)


def pack(s):
    r, c = iota((H, H), 0), iota((H, H), 1)
    s00, s01, s11 = s[:H, :H], s[:H, H:], s[H:, H:]
    tri = jnp.where(r >= c, s00, s11)
    d11 = jnp.sum(jnp.where(r == c, s11, 0.0), axis=0, keepdims=True)
    fold = lambda m: jnp.concatenate([m[: H // 2], m[H // 2 :]], 1)
    return fold(s01), fold(tri), d11


def unpack(b0, b1, d11):
    r, c = iota((H, H), 0), iota((H, H), 1)
    unfold = lambda m: jnp.concatenate([m[:, :H], m[:, H:]], 0)
    s01, tri = unfold(b0), unfold(b1)
    trit = tri.T
    s00 = jnp.where(r >= c, tri, trit)
    s11 = jnp.where(r == c, d11, jnp.where(r < c, tri, trit))
    top = jnp.concatenate([s00, s01], 1)
    low = jnp.concatenate([s01.T, s11], 1)
    return jnp.concatenate([top, low], 0)


def vec_block(c8, d11):
    d8 = jnp.broadcast_to(jnp.concatenate([jnp.zeros((1, H), F32), d11], 1), (8, N))
    return jnp.where(iota((8, N), 0) == 0, c8, d8)


def rows8(v):
    return jnp.broadcast_to(v, (8, N))


def kernel(dims, obs_ref, mask_ref, r_ref, m0_ref, fg_hbm, sg_hbm, a_hbm, q_hbm, p0_hbm,
           mean_ref, cov_ref,
           a_ref, q_ref, p0_ref, mb, gb, fi, si, ci, yb, yv, zb, zv, ex, by, byv, bz, bzv, sb, tb, jb, gm, lm,
           cf, cs, cc, pf, ps, pc, qf, qs, qc, hx, wy, ly, xa, xc, ca, cv, uf, rf, uc, fy, sy, fz, sz,
           send_sem, recv_sem, load_sem):
    nx, ny, nz = dims
    t = lax.axis_index("tm")
    c = lax.axis_index("col")
    o = 1 - c
    x = lax.rem(t, nx)
    y = lax.rem(t // nx, ny)
    z = t // (nx * ny)

    def at_x(d):
        return (t - x + lax.rem(x + d, nx), c)

    def at_y(d):
        return (t - y * nx + lax.rem(y + d, ny) * nx, c)

    def at_z(d):
        return (t - z * (nx * ny) + lax.rem(z + d, nz) * (nx * ny), c)

    sib = (t, o)
    rings = {"x": (at_x, x, nx), "y": (at_y, y, ny), "z": (at_z, z, nz)}

    def order(n):
        out = []
        for d in range(1, n // 2 + 1):
            out.append(d)
            if d != n - d:
                out.append(n - d)
        return out if n > 1 else []

    def load(i, src, dst):
        cp = pltpu.make_async_copy(src, dst, load_sem.at[i])
        cp.start()
        return cp

    barrier = pltpu.get_barrier_semaphore()
    peers = [sib]
    for at, _, n in rings.values():
        peers += [at(d) for d in range(1, n)]
    for dev in peers:
        pl.semaphore_signal(barrier, inc=1, device_id=dev, device_id_type=MESH)

    fg_load = load(0, fg_hbm, mb.at[x, c, pl.ds(0, H)])
    sg_load = load(1, sg_hbm, gb.at[x, c])
    other_loads = [load(2, a_hbm, a_ref), load(3, q_hbm, q_ref), load(4, p0_hbm, p0_ref)]

    count = [0]
    sent = []

    def slots(k):
        count[0] += k
        return count[0] - k

    def start(ref, sem, dev):
        cp = pltpu.make_async_remote_copy(
            src_ref=ref, dst_ref=ref, send_sem=send_sem.at[sem], recv_sem=recv_sem.at[sem],
            device_id=dev, device_id_type=MESH)
        cp.start()
        sent.append(cp)

    def arrived(ref, sem):
        pltpu.make_async_remote_copy(
            src_ref=ref, dst_ref=ref, send_sem=send_sem.at[sem], recv_sem=recv_sem.at[sem],
            device_id=sib, device_id_type=MESH).wait_recv()

    class Gather:
        def __init__(self, ring, buf):
            self.at, self.me, self.n = rings[ring]
            self.buf = buf
            self.s1, self.s2 = slots(self.n), slots(self.n)

        def source(self, d):
            return lax.rem(self.me + self.n - d, self.n)

        def send(self):
            for d in order(self.n):
                start(self.buf.at[self.me, c], self.s1 + d, self.at(d))

        def swap(self, d):
            if d:
                arrived(self.buf.at[self.source(d), c], self.s1 + d)
            start(self.buf.at[self.source(d), c], self.s2 + d, sib)

        def swapped(self, d):
            arrived(self.buf.at[self.source(d), o], self.s2 + d)

        def finish(self):
            for d in order(self.n):
                self.swap(d)
            for d in order(self.n):
                self.swapped(d)

    maybe_sent = []

    def maybe_start(cond, ref, sem, dev):
        def copy():
            return pltpu.make_async_remote_copy(
                src_ref=ref, dst_ref=ref, send_sem=send_sem.at[sem], recv_sem=recv_sem.at[sem],
                device_id=dev, device_id_type=MESH)

        @pl.when(cond)
        def _():
            copy().start()

        maybe_sent.append((cond, copy))

    class DownGather(Gather):
        def wanted(self, d):
            return (self.source(d) > self.me) & (self.source(d) < self.n - 1)

        def send(self):
            for d in order(self.n):
                to = lax.rem(self.me + d, self.n)
                cond = (to < self.me) & (self.me < self.n - 1)
                maybe_start(cond, self.buf.at[self.me, c], self.s1 + d, self.at(d))

        def finish(self):
            for d in order(self.n):
                @pl.when(self.wanted(d))
                def _():
                    arrived(self.buf.at[self.source(d), c], self.s1 + d)

                maybe_start(self.wanted(d), self.buf.at[self.source(d), c], self.s2 + d, sib)
            for d in order(self.n):
                @pl.when(self.wanted(d))
                def _():
                    arrived(self.buf.at[self.source(d), o], self.s2 + d)

    class SplitGather:
        def __init__(self, ring, buf, vec):
            self.at, self.me, self.n = rings[ring]
            self.buf, self.vec = buf, vec
            self.s1, self.s2, self.sv = slots(self.n), slots(self.n), slots(self.n)
            self.s3 = slots(self.n * nx)

        def source(self, d):
            return lax.rem(self.me + self.n - d, self.n)

        def send(self):
            for d in order(self.n):
                start(self.buf.at[self.me, c, x], self.s1 + d, self.at(d))
            for d in order(self.n):
                start(self.vec.at[self.me], self.sv + d, self.at(d))

        def forward(self):
            for d in order(self.n):
                k = self.source(d)
                arrived(self.buf.at[k, c, x], self.s1 + d)
                for e in order(nx):
                    start(self.buf.at[k, c, x], self.s3 + d * nx + e, at_x(e))

        def collect_one(self, d):
            k = self.source(d)
            for e in order(nx):
                arrived(self.buf.at[k, c, lax.rem(x + nx - e, nx)], self.s3 + d * nx + e)
            start(self.buf.at[k, c], self.s2 + d, sib)
            arrived(self.vec.at[k], self.sv + d)

        def collect(self):
            for d in order(self.n):
                self.collect_one(d)

        def unpacked(self, f_ref, s_ref):
            ds = order(self.n)
            for i in range(len(ds) + 1):
                if i < len(ds):
                    self.collect_one(ds[i])
                if i > 0:
                    self.swapped_one(ds[i - 1])
                    k = self.source(ds[i - 1])
                    f, s, _ = get_item(self.buf, self.vec, k)
                    f_ref[k] = f
                    s_ref[k] = s

        def swapped_one(self, d):
            arrived(self.buf.at[self.source(d), o], self.s2 + d)

        def swapped(self):
            for d in order(self.n):
                self.swapped_one(d)

    pr = H // nx
    sr = H // 2 // nx

    def put_item(buf, vec, k, f, s, c8):
        b0, b1, d11 = pack(s)
        for h, blk in ((0, b0), (1, b1)):
            for q in range(nx):
                buf[k, h, q, :pr] = f[h * H + q * pr : h * H + (q + 1) * pr]
                buf[k, h, q, pr:] = blk[q * sr : (q + 1) * sr]
        vec[k] = vec_block(c8, d11)

    def get_item(buf, vec, k):
        f = jnp.concatenate([buf[k, h, q, :pr] for h in range(2) for q in range(nx)], 0)
        b = [jnp.concatenate([buf[k, h, q, pr:] for q in range(nx)], 0) for h in range(2)]
        v = vec[k]
        return f, unpack(b[0], b[1], v[1:2, H:]), rows8(v[0:1])

    def put_sym(buf, vec, k, s, c8):
        b0, b1, d11 = pack(s)
        for h, blk in ((0, b0), (1, b1)):
            for q in range(nx):
                buf[k, h, q] = blk[q * sr : (q + 1) * sr]
        vec[k] = vec_block(c8, d11)

    def get_sym(buf, vec, k):
        b = [jnp.concatenate([buf[k, h, q] for q in range(nx)], 0) for h in range(2)]
        v = vec[k]
        return unpack(b[0], b[1], v[1:2, H:]), rows8(v[0:1])

    def whole(buf, k):
        return jnp.concatenate([buf[k, 0, :H], buf[k, 1, :H]], 0)

    mask = mask_ref[...].astype(F32)
    mb[x, c, H:] = rows8(obs_ref[...])
    fg_load.wait()
    mb[x, c, :H] = mb[x, c, :H] * mask
    pl.semaphore_wait(barrier, len(peers))
    m_ag, g_ag = Gather("x", mb), Gather("x", gb)
    m_ag.send()
    m_ag.swap(0)

    def step_item(d):
        k = m_ag.source(d)
        m = whole(mb, k)
        both = mm(m, jnp.concatenate([a_ref[...], q_ref[...]], 1))
        u = both[:, N:]
        v = u + m * r_ref[...] - q_ref[...]
        w = mm(jnp.concatenate([v, mb[k, c, H:]], 0), m, nt=True)
        fi[k] = a_ref[...] - both[:, :N]
        si[k] = q_ref[...] - u + w[:N]
        ci[k] = w[N:]

    for cp in other_loads:
        cp.wait()
    m_ag.swapped(0)
    step_item(0)
    for d in order(nx):
        m_ag.swap(d)
        if d == order(nx)[-1]:
            sg_load.wait()
            g_ag.swap(0)
            g_ag.send()
        m_ag.swapped(d)
        step_item(d)

    eye = jnp.where(iota((N, N), 0) == iota((N, N), 1), 1.0, 0.0).astype(F32)
    zero8 = jnp.zeros((8, N), F32)
    pf[...] = eye
    ps[...] = jnp.zeros((N, N), F32)
    pc[...] = zero8
    cf[...] = fi[0]
    cs[...] = si[0]
    cc[...] = ci[0]

    def chain(steps, me, item, f_ref, s_ref, c_ref):
        def body(k, carry):
            @pl.when(me == k)
            def _():
                f_ref[...] = cf[...]
                s_ref[...] = cs[...]
                c_ref[...] = cc[...]

            f, s, c8 = item(k)
            ns, nc = cong(f, cs[...], cc[...])
            cf[...] = mm(f, cf[...])
            cs[...] = ns + s
            cc[...] = nc + c8
            return carry

        lax.fori_loop(1, steps, body, 0)

    chain(nx, x, lambda k: (fi[k], si[k], ci[k]), pf, ps, pc)

    y_ag = SplitGather("y", yb, yv)
    put_item(yb, yv, y, cf[...], cs[...], cc[...])
    y_ag.send()
    fy[y] = cf[...]
    sy[y] = cs[...]

    g_ag.swapped(0)
    g_ag.finish()
    hx[...] = whole(gb, nx - 1)
    cf[...] = whole(gb, nx - 1)

    def back_x(i, carry):
        k = nx - 2 - i
        cf[...] = mm(whole(gb, k), cf[...])

        @pl.when(x == k)
        def _():
            hx[...] = cf[...]

        return carry

    lax.fori_loop(0, nx - 1, back_x, 0)
    gm[y, 0] = cf[:H]
    gm[y, 1] = cf[H:]

    y_ag.forward()
    gm_ag = Gather("y", gm)
    gm_ag.send()
    y_ag.unpacked(fy, sy)

    cf[...] = fy[ny - 1]
    cs[...] = sy[ny - 1]
    cc[...] = rows8(yv[ny - 1, 0:1])
    rf[...] = eye
    uf[...] = jnp.zeros((N, N), F32)
    uc[...] = zero8

    def add_term():
        term = mm(jnp.concatenate([uf[...], uc[...]], 0), rf[...], nt=True)
        cs[...] += term[:N]
        cc[...] += term[N:]

    def total_y(i, carry):
        k = ny - 1 - i
        r = cf[...]
        both = mm(r, jnp.concatenate([fy[k], sy[k]], 1))
        add_term()
        rf[...] = r
        uf[...] = both[:, N:]
        uc[...] = rows8(yv[k, 0:1])
        cf[...] = both[:, :N]
        return carry

    lax.fori_loop(1, ny, total_y, 0)
    add_term()

    z_ag = SplitGather("z", zb, zv)
    put_item(zb, zv, z, cf[...], cs[...], cc[...])
    z_ag.send()

    qf[...] = eye
    qs[...] = jnp.zeros((N, N), F32)
    qc[...] = zero8

    def before(f, s, c8):
        ns, nc = cong(f, qs[...], qc[...])
        qf[...] = mm(f, qf[...])
        qs[...] = ns + s
        qc[...] = nc + c8

    def before_y(k, carry):
        before(fy[k], sy[k], rows8(yv[k, 0:1]))
        return carry

    lax.fori_loop(0, y, before_y, 0)
    before(pf[...], ps[...], pc[...])
    z_ag.forward()

    gm_ag.finish()
    cf[...] = eye

    def map_y(k, carry):
        @pl.when(y == k)
        def _():
            ly[...] = cf[...]

        cf[...] = mm(cf[...], whole(gm, k))
        return carry

    lax.fori_loop(0, ny, map_y, 0)
    lm[z, 0] = cf[:H]
    lm[z, 1] = cf[H:]
    lm_ag = DownGather("z", lm)
    lm_ag.send()

    z_ag.unpacked(fz, sz)
    cs[...] = p0_ref[...]
    cc[...] = rows8(m0_ref[...])

    def carry_in(k, carry):
        ns, nc = cong(fz[k], cs[...], cc[...])
        cs[...] = ns + sz[k]
        cc[...] = nc + rows8(zv[k, 0:1])
        return carry

    lax.fori_loop(0, z, carry_in, 0)
    p_prev, m_prev = cong(qf[...], cs[...], cc[...])
    p_prev = p_prev + qs[...]
    m_prev = m_prev + qc[...]

    pred, am = cong(a_ref[...], p_prev, m_prev)
    pred = pred + q_ref[...]
    m = whole(mb, x)
    w = mm(m, pred)
    v = w + m * r_ref[...] - pred
    ee = mm(jnp.concatenate([v, rows8(obs_ref[...]) - am], 0), m, nt=True)
    e_cov = ee[:N] - w
    e_vec = ee[N:]
    b0, b1, d11 = pack(e_cov)
    vb = vec_block(e_vec, d11)
    for h, blk in ((0, b0), (1, b1)):
        ex[x, h, : H // 2] = blk
        ex[x, h, H // 2 :] = vb
    ps[...] = pred
    pc[...] = am

    e_ag = Gather("x", ex)
    e_ag.send()
    cf[...] = eye

    def back_y_map(i, carry):
        k = ny - 1 - i

        @pl.when(y == k)
        def _():
            wy[...] = cf[...]

        cf[...] = mm(whole(gm, k), cf[...])
        return carry

    lax.fori_loop(0, ny - 1, back_y_map, 0)

    @pl.when(y == 0)
    def _():
        wy[...] = cf[...]

    rf[...] = mm(hx[...], wy[...])
    e_ag.finish()

    def get_e(k):
        vb = ex[k, c, H // 2 :]
        return unpack(ex[k, 0, : H // 2], ex[k, 1, : H // 2], vb[1:2, H:]), rows8(vb[0:1])

    s, c8 = get_e(nx - 1)
    xa[...] = s
    xc[...] = c8
    cs[...] = s
    cc[...] = c8

    def back_x_cov(i, carry):
        k = nx - 2 - i
        s, c8 = get_e(k)
        ns, nc = cong(whole(gb, k), cs[...], cc[...])
        cs[...] = ns + s
        cc[...] = nc + c8

        @pl.when(x == k)
        def _():
            xa[...] = cs[...]
            xc[...] = cc[...]

        return carry

    lax.fori_loop(0, nx - 1, back_x_cov, 0)

    ns, nc = cong(ly[...], cs[...], cc[...])
    b0, b1, d11 = pack(ns)
    for h, blk in ((0, b0), (1, b1)):
        for q in range(nx):
            tb[h, q] = blk[q * sr : (q + 1) * sr]
    sb[y, :sr] = tb[c, x]
    sb[y, sr:] = vec_block(nc, d11)
    s_slots = slots(ny)
    for d in order(ny):
        start(sb.at[y], s_slots + d, at_y(d))
    by_ag = SplitGather("y", by, byv)
    put_sym(by, byv, y, cs[...], cc[...])
    by_ag.send()

    lm_ag.finish()
    cf[...] = rf[...]

    def map_z(k, carry):
        jb[k] = cf[...]

        @pl.when(k < nz - 1)
        def _():
            cf[...] = mm(cf[...], whole(lm, k))

        return carry

    lax.fori_loop(z + 1, nz, map_z, 0)

    for d in order(ny):
        arrived(sb.at[by_ag.source(d)], s_slots + d)
    total = sb[0]
    for k in range(1, ny):
        total = total + sb[k]
    bz_ag = SplitGather("z", bz, bzv)
    bz[z, c, x] = total[:sr]
    bzv[z] = total[sr:]
    bz_ag.send()

    by_ag.forward()
    by_ag.collect()
    bz_ag.forward()
    by_ag.swapped()
    ca[...] = jnp.zeros((N, N), F32)
    cv[...] = zero8

    def back_y_cov(i, carry):
        k = ny - 1 - i
        s, c8 = get_sym(by, byv, k)
        ns, nc = cong(whole(gm, k), ca[...], cv[...])
        ca[...] = ns + s
        cv[...] = nc + c8
        return carry

    lax.fori_loop(0, ny - 1 - y, back_y_cov, 0)
    ns, nc = cong(hx[...], ca[...], cv[...])
    xa[...] = xa[...] + ns + ps[...]
    xc[...] = xc[...] + nc + pc[...]

    bz_ag.collect()
    for d in order(nz):
        k = bz_ag.source(d)
        bz_ag.swapped_one(d)

        @pl.when(k > z)
        def _():
            s, c8 = get_sym(bz, bzv, k)
            ns, nc = cong(jb[k], s, c8)
            xa[...] += ns
            xc[...] += nc

    cov_ref[...] = xa[pl.ds(pl.multiple_of(c * H, H), H)]
    mean_ref[...] = jnp.where(c == 0, xc[0:1, :H], xc[0:1, H:])
    for cp in sent:
        cp.wait_send()
    for cond, copy in maybe_sent:
        @pl.when(cond)
        def _():
            copy().wait_send()


def shards(steps, observations, sensor_mask, filter_gain, smoother_gain, dynamics, process_noise,
           sensor_noise, initial_mean, initial_cov):
    dims = grid_dims(steps)
    nx, ny, nz = dims
    mat = pltpu.VMEM((N, N), F32)
    vec = pltpu.VMEM((8, N), F32)
    buf = lambda *s: pltpu.VMEM(s + (N,), F32)
    n_sem = 3 * nx * 2 + (ny + nz) * 2 + 2 * (ny + nz) * (3 + nx) + ny
    vmem = pl.BlockSpec(memory_space=pltpu.VMEM)
    hbm = pl.BlockSpec(memory_space=pltpu.HBM)
    sr = H // 2 // nx
    mean, cov = pl.pallas_call(
        functools.partial(kernel, dims),
        out_shape=(jax.ShapeDtypeStruct((1, H), F32), jax.ShapeDtypeStruct((H, N), F32)),
        in_specs=[vmem] * 4 + [hbm] * 5,
        out_specs=(vmem, vmem),
        scratch_shapes=[
            mat, mat, mat,
            buf(nx, 2, H + 8), buf(nx, 2, H),
            buf(nx, N), buf(nx, N), buf(nx, 8),
            buf(ny, 2, nx, (H + H // 2) // nx), buf(ny, 8),
            buf(nz, 2, nx, (H + H // 2) // nx), buf(nz, 8),
            buf(nx, 2, H // 2 + 8),
            buf(ny, 2, nx, H // 2 // nx), buf(ny, 8),
            buf(nz, 2, nx, H // 2 // nx), buf(nz, 8),
            buf(ny, sr + 8), buf(2, nx, sr), buf(nz, N), buf(ny, 2, H), buf(nz, 2, H),
            mat, mat, vec, mat, mat, vec, mat, mat, vec, mat, mat, mat, mat, vec, mat, vec,
            mat, mat, vec, buf(ny, N), buf(ny, N), buf(nz, N), buf(nz, N),
            pltpu.SemaphoreType.DMA((n_sem,)), pltpu.SemaphoreType.DMA((n_sem,)),
            pltpu.SemaphoreType.DMA((5,)),
        ],
        compiler_params=pltpu.CompilerParams(
            collective_id=0, has_side_effects=True, vmem_limit_bytes=60 << 20),
    )(observations[0], sensor_mask[0], sensor_noise, initial_mean, filter_gain[0, 0],
      smoother_gain[0, 0], dynamics[0], process_noise[0], initial_cov[0])
    return mean[None], cov[None, None]


def solution(mesh):
    return jax.shard_map(
        functools.partial(shards, mesh.shape["tm"]),
        mesh=mesh,
        in_specs=(
            P(None, "tm", None),
            P(None, "tm", None),
            P(None, "tm", "col", None),
            P(None, "tm", "col", None),
            P(),
            P(),
            P(),
            P(),
            P(),
        ),
        out_specs=(P(None, "tm", "col"), P(None, "tm", "col", None)),
        check_vma=False,
    )
```

```python
import functools

import jax
import jax.numpy as jnp
from jax import lax
from jax.experimental import pallas as pl
from jax.experimental.pallas import tpu as pltpu
from jax.sharding import PartitionSpec as P

MESH = pl.DeviceIdType.MESH
F32 = jnp.float32
N = 256
H = 128


def grid_dims(steps):
    return {256: (4, 8, 8), 8: (2, 2, 2), 4: (2, 2, 1)}[steps]


def parts(a):
    hi = a.astype(jnp.bfloat16)
    lo = (a - hi.astype(F32)).astype(jnp.bfloat16)
    return hi, lo


def mm(a, b, nt=False):
    ah, al = parts(a)
    bh, bl = parts(b)
    dims = (((1,), (1 if nt else 0,)), ((), ()))
    dot = functools.partial(lax.dot_general, dimension_numbers=dims, preferred_element_type=F32)
    return dot(ah, bh) + (dot(ah, bl) + dot(al, bh))


def cong(f, s, c8):
    t = mm(jnp.concatenate([s, c8], 0), f, nt=True)
    return mm(f, t[:N]), t[N:]


def iota(shape, dim):
    return lax.broadcasted_iota(jnp.int32, shape, dim)


def pack(s):
    r, c = iota((H, H), 0), iota((H, H), 1)
    s00, s01, s11 = s[:H, :H], s[:H, H:], s[H:, H:]
    tri = jnp.where(r >= c, s00, s11)
    d11 = jnp.sum(jnp.where(r == c, s11, 0.0), axis=0, keepdims=True)
    fold = lambda m: jnp.concatenate([m[: H // 2], m[H // 2 :]], 1)
    return fold(s01), fold(tri), d11


def unpack(b0, b1, d11):
    r, c = iota((H, H), 0), iota((H, H), 1)
    unfold = lambda m: jnp.concatenate([m[:, :H], m[:, H:]], 0)
    s01, tri = unfold(b0), unfold(b1)
    trit = tri.T
    s00 = jnp.where(r >= c, tri, trit)
    s11 = jnp.where(r == c, d11, jnp.where(r < c, tri, trit))
    top = jnp.concatenate([s00, s01], 1)
    low = jnp.concatenate([s01.T, s11], 1)
    return jnp.concatenate([top, low], 0)


def vec_block(c8, d11):
    d8 = jnp.broadcast_to(jnp.concatenate([jnp.zeros((1, H), F32), d11], 1), (8, N))
    return jnp.where(iota((8, N), 0) == 0, c8, d8)


def rows8(v):
    return jnp.broadcast_to(v, (8, N))


def kernel(dims, obs_ref, mask_ref, r_ref, m0_ref, fg_hbm, sg_hbm, a_hbm, q_hbm, p0_hbm,
           mean_ref, cov_ref,
           a_ref, q_ref, p0_ref, mb, gb, fi, si, ci, yb, yv, zb, zv, ex, by, byv, bz, bzv, sb, tb, jb, gm, lm,
           cf, cs, cc, pf, ps, pc, qf, qs, qc, hx, wy, ly, xa, xc, ca, cv, uf, rf, uc, fy, sy, fz, sz,
           send_sem, recv_sem, load_sem):
    nx, ny, nz = dims
    t = lax.axis_index("tm")
    c = lax.axis_index("col")
    o = 1 - c
    x = lax.rem(t, nx)
    y = lax.rem(t // nx, ny)
    z = t // (nx * ny)

    def at_x(d):
        return (t - x + lax.rem(x + d, nx), c)

    def at_y(d):
        return (t - y * nx + lax.rem(y + d, ny) * nx, c)

    def at_z(d):
        return (t - z * (nx * ny) + lax.rem(z + d, nz) * (nx * ny), c)

    sib = (t, o)
    rings = {"x": (at_x, x, nx), "y": (at_y, y, ny), "z": (at_z, z, nz)}

    def order(n):
        out = []
        for d in range(1, n // 2 + 1):
            out.append(d)
            if d != n - d:
                out.append(n - d)
        return out if n > 1 else []

    def load(i, src, dst):
        cp = pltpu.make_async_copy(src, dst, load_sem.at[i])
        cp.start()
        return cp

    barrier = pltpu.get_barrier_semaphore()
    peers = [sib]
    for at, _, n in rings.values():
        peers += [at(d) for d in range(1, n)]
    for dev in peers:
        pl.semaphore_signal(barrier, inc=1, device_id=dev, device_id_type=MESH)

    fg_load = load(0, fg_hbm, mb.at[x, c, pl.ds(0, H)])
    sg_load = load(1, sg_hbm, gb.at[x, c])
    other_loads = [load(2, a_hbm, a_ref), load(3, q_hbm, q_ref), load(4, p0_hbm, p0_ref)]

    count = [0]
    sent = []

    def slots(k):
        count[0] += k
        return count[0] - k

    def start(ref, sem, dev):
        cp = pltpu.make_async_remote_copy(
            src_ref=ref, dst_ref=ref, send_sem=send_sem.at[sem], recv_sem=recv_sem.at[sem],
            device_id=dev, device_id_type=MESH)
        cp.start()
        sent.append(cp)

    def arrived(ref, sem):
        pltpu.make_async_remote_copy(
            src_ref=ref, dst_ref=ref, send_sem=send_sem.at[sem], recv_sem=recv_sem.at[sem],
            device_id=sib, device_id_type=MESH).wait_recv()

    class Gather:
        def __init__(self, ring, buf):
            self.at, self.me, self.n = rings[ring]
            self.buf = buf
            self.s1, self.s2 = slots(self.n), slots(self.n)

        def source(self, d):
            return lax.rem(self.me + self.n - d, self.n)

        def send(self):
            for d in order(self.n):
                start(self.buf.at[self.me, c], self.s1 + d, self.at(d))

        def swap(self, d):
            if d:
                arrived(self.buf.at[self.source(d), c], self.s1 + d)
            start(self.buf.at[self.source(d), c], self.s2 + d, sib)

        def swapped(self, d):
            arrived(self.buf.at[self.source(d), o], self.s2 + d)

        def finish(self):
            for d in order(self.n):
                self.swap(d)
            for d in order(self.n):
                self.swapped(d)

    maybe_sent = []

    def maybe_start(cond, ref, sem, dev):
        def copy():
            return pltpu.make_async_remote_copy(
                src_ref=ref, dst_ref=ref, send_sem=send_sem.at[sem], recv_sem=recv_sem.at[sem],
                device_id=dev, device_id_type=MESH)

        @pl.when(cond)
        def _():
            copy().start()

        maybe_sent.append((cond, copy))

    class DownGather(Gather):
        def wanted(self, d):
            return (self.source(d) > self.me) & (self.source(d) < self.n - 1)

        def send(self):
            for d in order(self.n):
                to = lax.rem(self.me + d, self.n)
                cond = (to < self.me) & (self.me < self.n - 1)
                maybe_start(cond, self.buf.at[self.me, c], self.s1 + d, self.at(d))

        def finish(self):
            for d in order(self.n):
                @pl.when(self.wanted(d))
                def _():
                    arrived(self.buf.at[self.source(d), c], self.s1 + d)

                maybe_start(self.wanted(d), self.buf.at[self.source(d), c], self.s2 + d, sib)
            for d in order(self.n):
                @pl.when(self.wanted(d))
                def _():
                    arrived(self.buf.at[self.source(d), o], self.s2 + d)

    class SplitGather:
        def __init__(self, ring, buf, vec):
            self.at, self.me, self.n = rings[ring]
            self.buf, self.vec = buf, vec
            self.s1, self.s2, self.sv = slots(self.n), slots(self.n), slots(self.n)
            self.s3 = slots(self.n * nx)

        def source(self, d):
            return lax.rem(self.me + self.n - d, self.n)

        def send(self):
            for d in order(self.n):
                start(self.buf.at[self.me, c, x], self.s1 + d, self.at(d))
            for d in order(self.n):
                start(self.vec.at[self.me], self.sv + d, self.at(d))

        def forward(self):
            for d in order(self.n):
                k = self.source(d)
                arrived(self.buf.at[k, c, x], self.s1 + d)
                for e in order(nx)[::-1]:
                    start(self.buf.at[k, c, x], self.s3 + d * nx + e, at_x(e))

        def collect_one(self, d):
            k = self.source(d)
            for e in order(nx):
                arrived(self.buf.at[k, c, lax.rem(x + nx - e, nx)], self.s3 + d * nx + e)
            start(self.buf.at[k, c], self.s2 + d, sib)
            arrived(self.vec.at[k], self.sv + d)

        def collect(self):
            for d in order(self.n):
                self.collect_one(d)

        def unpacked(self, f_ref, s_ref):
            ds = order(self.n)
            for i in range(len(ds) + 1):
                if i < len(ds):
                    self.collect_one(ds[i])
                if i > 0:
                    self.swapped_one(ds[i - 1])
                    k = self.source(ds[i - 1])
                    f, s, _ = get_item(self.buf, self.vec, k)
                    f_ref[k] = f
                    s_ref[k] = s

        def swapped_one(self, d):
            arrived(self.buf.at[self.source(d), o], self.s2 + d)

        def swapped(self):
            for d in order(self.n):
                self.swapped_one(d)

    pr = H // nx
    sr = H // 2 // nx

    def put_item(buf, vec, k, f, s, c8):
        b0, b1, d11 = pack(s)
        for h, blk in ((0, b0), (1, b1)):
            for q in range(nx):
                buf[k, h, q, :pr] = f[h * H + q * pr : h * H + (q + 1) * pr]
                buf[k, h, q, pr:] = blk[q * sr : (q + 1) * sr]
        vec[k] = vec_block(c8, d11)

    def get_item(buf, vec, k):
        f = jnp.concatenate([buf[k, h, q, :pr] for h in range(2) for q in range(nx)], 0)
        b = [jnp.concatenate([buf[k, h, q, pr:] for q in range(nx)], 0) for h in range(2)]
        v = vec[k]
        return f, unpack(b[0], b[1], v[1:2, H:]), rows8(v[0:1])

    def put_sym(buf, vec, k, s, c8):
        b0, b1, d11 = pack(s)
        for h, blk in ((0, b0), (1, b1)):
            for q in range(nx):
                buf[k, h, q] = blk[q * sr : (q + 1) * sr]
        vec[k] = vec_block(c8, d11)

    def get_sym(buf, vec, k):
        b = [jnp.concatenate([buf[k, h, q] for q in range(nx)], 0) for h in range(2)]
        v = vec[k]
        return unpack(b[0], b[1], v[1:2, H:]), rows8(v[0:1])

    def whole(buf, k):
        return jnp.concatenate([buf[k, 0, :H], buf[k, 1, :H]], 0)

    mask = mask_ref[...].astype(F32)
    mb[x, c, H:] = rows8(obs_ref[...])
    fg_load.wait()
    mb[x, c, :H] = mb[x, c, :H] * mask
    pl.semaphore_wait(barrier, len(peers))
    m_ag, g_ag = Gather("x", mb), Gather("x", gb)
    m_ag.send()
    m_ag.swap(0)

    def step_item(d):
        k = m_ag.source(d)
        m = whole(mb, k)
        both = mm(m, jnp.concatenate([a_ref[...], q_ref[...]], 1))
        u = both[:, N:]
        v = u + m * r_ref[...] - q_ref[...]
        w = mm(jnp.concatenate([v, mb[k, c, H:]], 0), m, nt=True)
        fi[k] = a_ref[...] - both[:, :N]
        si[k] = q_ref[...] - u + w[:N]
        ci[k] = w[N:]

    for cp in other_loads:
        cp.wait()
    m_ag.swapped(0)
    step_item(0)
    for d in order(nx):
        m_ag.swap(d)
        if d == order(nx)[-1]:
            sg_load.wait()
            g_ag.swap(0)
            g_ag.send()
        m_ag.swapped(d)
        step_item(d)

    eye = jnp.where(iota((N, N), 0) == iota((N, N), 1), 1.0, 0.0).astype(F32)
    zero8 = jnp.zeros((8, N), F32)
    pf[...] = eye
    ps[...] = jnp.zeros((N, N), F32)
    pc[...] = zero8
    cf[...] = fi[0]
    cs[...] = si[0]
    cc[...] = ci[0]

    def chain(steps, me, item, f_ref, s_ref, c_ref):
        def body(k, carry):
            @pl.when(me == k)
            def _():
                f_ref[...] = cf[...]
                s_ref[...] = cs[...]
                c_ref[...] = cc[...]

            f, s, c8 = item(k)
            ns, nc = cong(f, cs[...], cc[...])
            cf[...] = mm(f, cf[...])
            cs[...] = ns + s
            cc[...] = nc + c8
            return carry

        lax.fori_loop(1, steps, body, 0)

    chain(nx, x, lambda k: (fi[k], si[k], ci[k]), pf, ps, pc)

    y_ag = SplitGather("y", yb, yv)
    put_item(yb, yv, y, cf[...], cs[...], cc[...])
    y_ag.send()
    fy[y] = cf[...]
    sy[y] = cs[...]

    g_ag.swapped(0)
    g_ag.finish()
    hx[...] = whole(gb, nx - 1)
    cf[...] = whole(gb, nx - 1)

    def back_x(i, carry):
        k = nx - 2 - i
        cf[...] = mm(whole(gb, k), cf[...])

        @pl.when(x == k)
        def _():
            hx[...] = cf[...]

        return carry

    lax.fori_loop(0, nx - 1, back_x, 0)
    gm[y, 0] = cf[:H]
    gm[y, 1] = cf[H:]

    y_ag.forward()
    gm_ag = Gather("y", gm)
    gm_ag.send()
    y_ag.unpacked(fy, sy)

    cf[...] = fy[ny - 1]
    cs[...] = sy[ny - 1]
    cc[...] = rows8(yv[ny - 1, 0:1])
    rf[...] = eye
    uf[...] = jnp.zeros((N, N), F32)
    uc[...] = zero8

    def add_term():
        term = mm(jnp.concatenate([uf[...], uc[...]], 0), rf[...], nt=True)
        cs[...] += term[:N]
        cc[...] += term[N:]

    def total_y(i, carry):
        k = ny - 1 - i
        r = cf[...]
        both = mm(r, jnp.concatenate([fy[k], sy[k]], 1))
        add_term()
        rf[...] = r
        uf[...] = both[:, N:]
        uc[...] = rows8(yv[k, 0:1])
        cf[...] = both[:, :N]
        return carry

    lax.fori_loop(1, ny, total_y, 0)
    add_term()

    z_ag = SplitGather("z", zb, zv)
    put_item(zb, zv, z, cf[...], cs[...], cc[...])
    z_ag.send()

    qf[...] = eye
    qs[...] = jnp.zeros((N, N), F32)
    qc[...] = zero8

    def before(f, s, c8):
        ns, nc = cong(f, qs[...], qc[...])
        qf[...] = mm(f, qf[...])
        qs[...] = ns + s
        qc[...] = nc + c8

    def before_y(k, carry):
        before(fy[k], sy[k], rows8(yv[k, 0:1]))
        return carry

    lax.fori_loop(0, y, before_y, 0)
    before(pf[...], ps[...], pc[...])
    z_ag.forward()

    gm_ag.finish()
    cf[...] = eye

    def map_y(k, carry):
        @pl.when(y == k)
        def _():
            ly[...] = cf[...]

        cf[...] = mm(cf[...], whole(gm, k))
        return carry

    lax.fori_loop(0, ny, map_y, 0)
    lm[z, 0] = cf[:H]
    lm[z, 1] = cf[H:]
    lm_ag = DownGather("z", lm)
    lm_ag.send()

    z_ag.unpacked(fz, sz)
    cs[...] = p0_ref[...]
    cc[...] = rows8(m0_ref[...])

    def carry_in(k, carry):
        ns, nc = cong(fz[k], cs[...], cc[...])
        cs[...] = ns + sz[k]
        cc[...] = nc + rows8(zv[k, 0:1])
        return carry

    lax.fori_loop(0, z, carry_in, 0)
    p_prev, m_prev = cong(qf[...], cs[...], cc[...])
    p_prev = p_prev + qs[...]
    m_prev = m_prev + qc[...]

    pred, am = cong(a_ref[...], p_prev, m_prev)
    pred = pred + q_ref[...]
    m = whole(mb, x)
    w = mm(m, pred)
    v = w + m * r_ref[...] - pred
    ee = mm(jnp.concatenate([v, rows8(obs_ref[...]) - am], 0), m, nt=True)
    e_cov = ee[:N] - w
    e_vec = ee[N:]
    b0, b1, d11 = pack(e_cov)
    vb = vec_block(e_vec, d11)
    for h, blk in ((0, b0), (1, b1)):
        ex[x, h, : H // 2] = blk
        ex[x, h, H // 2 :] = vb
    ps[...] = pred
    pc[...] = am

    e_ag = Gather("x", ex)
    e_ag.send()
    cf[...] = eye

    def back_y_map(i, carry):
        k = ny - 1 - i

        @pl.when(y == k)
        def _():
            wy[...] = cf[...]

        cf[...] = mm(whole(gm, k), cf[...])
        return carry

    lax.fori_loop(0, ny - 1, back_y_map, 0)

    @pl.when(y == 0)
    def _():
        wy[...] = cf[...]

    rf[...] = mm(hx[...], wy[...])
    e_ag.finish()

    def get_e(k):
        vb = ex[k, c, H // 2 :]
        return unpack(ex[k, 0, : H // 2], ex[k, 1, : H // 2], vb[1:2, H:]), rows8(vb[0:1])

    s, c8 = get_e(nx - 1)
    xa[...] = s
    xc[...] = c8
    cs[...] = s
    cc[...] = c8

    def back_x_cov(i, carry):
        k = nx - 2 - i
        s, c8 = get_e(k)
        ns, nc = cong(whole(gb, k), cs[...], cc[...])
        cs[...] = ns + s
        cc[...] = nc + c8

        @pl.when(x == k)
        def _():
            xa[...] = cs[...]
            xc[...] = cc[...]

        return carry

    lax.fori_loop(0, nx - 1, back_x_cov, 0)

    ns, nc = cong(ly[...], cs[...], cc[...])
    b0, b1, d11 = pack(ns)
    for h, blk in ((0, b0), (1, b1)):
        for q in range(nx):
            tb[h, q] = blk[q * sr : (q + 1) * sr]
    sb[y, :sr] = tb[c, x]
    sb[y, sr:] = vec_block(nc, d11)
    s_slots = slots(ny)
    for d in order(ny):
        start(sb.at[y], s_slots + d, at_y(d))
    by_ag = SplitGather("y", by, byv)
    put_sym(by, byv, y, cs[...], cc[...])
    by_ag.send()

    lm_ag.finish()
    cf[...] = rf[...]

    def map_z(k, carry):
        jb[k] = cf[...]

        @pl.when(k < nz - 1)
        def _():
            cf[...] = mm(cf[...], whole(lm, k))

        return carry

    lax.fori_loop(z + 1, nz, map_z, 0)

    for d in order(ny):
        arrived(sb.at[by_ag.source(d)], s_slots + d)
    total = sb[0]
    for k in range(1, ny):
        total = total + sb[k]
    bz_ag = SplitGather("z", bz, bzv)
    bz[z, c, x] = total[:sr]
    bzv[z] = total[sr:]
    bz_ag.send()

    by_ag.forward()
    by_ag.collect()
    bz_ag.forward()
    by_ag.swapped()
    ca[...] = jnp.zeros((N, N), F32)
    cv[...] = zero8

    def back_y_cov(i, carry):
        k = ny - 1 - i
        s, c8 = get_sym(by, byv, k)
        ns, nc = cong(whole(gm, k), ca[...], cv[...])
        ca[...] = ns + s
        cv[...] = nc + c8
        return carry

    lax.fori_loop(0, ny - 1 - y, back_y_cov, 0)
    ns, nc = cong(hx[...], ca[...], cv[...])
    xa[...] = xa[...] + ns + ps[...]
    xc[...] = xc[...] + nc + pc[...]

    bz_ag.collect()
    for d in order(nz):
        k = bz_ag.source(d)
        bz_ag.swapped_one(d)

        @pl.when(k > z)
        def _():
            s, c8 = get_sym(bz, bzv, k)
            ns, nc = cong(jb[k], s, c8)
            xa[...] += ns
            xc[...] += nc

    cov_ref[...] = xa[pl.ds(pl.multiple_of(c * H, H), H)]
    mean_ref[...] = jnp.where(c == 0, xc[0:1, :H], xc[0:1, H:])
    for cp in sent:
        cp.wait_send()
    for cond, copy in maybe_sent:
        @pl.when(cond)
        def _():
            copy().wait_send()


def shards(steps, observations, sensor_mask, filter_gain, smoother_gain, dynamics, process_noise,
           sensor_noise, initial_mean, initial_cov):
    dims = grid_dims(steps)
    nx, ny, nz = dims
    mat = pltpu.VMEM((N, N), F32)
    vec = pltpu.VMEM((8, N), F32)
    buf = lambda *s: pltpu.VMEM(s + (N,), F32)
    n_sem = 3 * nx * 2 + (ny + nz) * 2 + 2 * (ny + nz) * (3 + nx) + ny
    vmem = pl.BlockSpec(memory_space=pltpu.VMEM)
    hbm = pl.BlockSpec(memory_space=pltpu.HBM)
    sr = H // 2 // nx
    mean, cov = pl.pallas_call(
        functools.partial(kernel, dims),
        out_shape=(jax.ShapeDtypeStruct((1, H), F32), jax.ShapeDtypeStruct((H, N), F32)),
        in_specs=[vmem] * 4 + [hbm] * 5,
        out_specs=(vmem, vmem),
        scratch_shapes=[
            mat, mat, mat,
            buf(nx, 2, H + 8), buf(nx, 2, H),
            buf(nx, N), buf(nx, N), buf(nx, 8),
            buf(ny, 2, nx, (H + H // 2) // nx), buf(ny, 8),
            buf(nz, 2, nx, (H + H // 2) // nx), buf(nz, 8),
            buf(nx, 2, H // 2 + 8),
            buf(ny, 2, nx, H // 2 // nx), buf(ny, 8),
            buf(nz, 2, nx, H // 2 // nx), buf(nz, 8),
            buf(ny, sr + 8), buf(2, nx, sr), buf(nz, N), buf(ny, 2, H), buf(nz, 2, H),
            mat, mat, vec, mat, mat, vec, mat, mat, vec, mat, mat, mat, mat, vec, mat, vec,
            mat, mat, vec, buf(ny, N), buf(ny, N), buf(nz, N), buf(nz, N),
            pltpu.SemaphoreType.DMA((n_sem,)), pltpu.SemaphoreType.DMA((n_sem,)),
            pltpu.SemaphoreType.DMA((5,)),
        ],
        compiler_params=pltpu.CompilerParams(
            collective_id=0, has_side_effects=True, vmem_limit_bytes=60 << 20),
    )(observations[0], sensor_mask[0], sensor_noise, initial_mean, filter_gain[0, 0],
      smoother_gain[0, 0], dynamics[0], process_noise[0], initial_cov[0])
    return mean[None], cov[None, None]


def solution(mesh):
    return jax.shard_map(
        functools.partial(shards, mesh.shape["tm"]),
        mesh=mesh,
        in_specs=(
            P(None, "tm", None),
            P(None, "tm", None),
            P(None, "tm", "col", None),
            P(None, "tm", "col", None),
            P(),
            P(),
            P(),
            P(),
            P(),
        ),
        out_specs=(P(None, "tm", "col"), P(None, "tm", "col", None)),
        check_vma=False,
    )
```
